768 devices in a mesh: group: 12 (over z), tensor: 64 (over x, y, core).
Axes of the slice: x: 4, y: 8, z: 12, core: 2. Of those that a mesh axis runs over, the one named last changes fastest.
Arguments:
- hidden: bfloat16 [12, 256, 14336], P('group', None, 'tensor'), may hold values from -6 to 6
- weights: bfloat16 [12, 14336, 4096], P('group', 'tensor'), may hold values from -0.125 to 0.125
- target: bfloat16 [12, 256, 4096], P('group', None, 'tensor'), may hold values from -6 to 6
- module: int32 [12, 1], replicated, may hold values from 0 to 3
- counts: int32 [12], replicated, may hold values from 1 to 256, 1664 in all
Outputs:
- update: bfloat16 [12, 14336, 4096], P('group', 'tensor')
The draws below stay inside these ranges and needn't reach their ends.
Inputs may be any that keep to these rules, and one draw needn't show every extreme that they name: Every module number is used by at least one path.
All inputs are finite; a program needn't handle non-finite values.
Results may differ from the reference program's by a relative error of at most 0.0057.
Values may be sent and summed in bfloat16 or wider, within the bound.
A program may use at most 32 MiB of HBM per device.

```python
import math
import jax
import jax.numpy as jnp
import numpy as np
from jax import lax

D = 4096
FF = 14336
TOK = 256
PATHS = 12
MODS = 4


def spiked(values, key, source, target, shards_of, factor):
    owner, partner = [(jnp.arange(values.shape[position]) // (values.shape[position] // shards_of)).reshape([-1 if axis == position else 1 for axis in range(values.ndim)]) for position in (source, target)]
    chosen = jax.random.permutation(key, shards_of)[partner]
    strong = (owner == chosen) | (owner == (partner + shards_of // 2) % shards_of)
    return jnp.where(strong, factor * values, values)


def block_scale(key, dims, shards, smallest, top_value):
    loudness = 1.0
    for position, parts in shards:
        steps = jax.random.uniform(jax.random.fold_in(jax.random.fold_in(key, 6), position), (parts,), jnp.float32, smallest / len(shards), top_value / len(shards))
        loudness = loudness * jnp.repeat(jnp.exp(steps), dims[position] // parts).reshape((-1,) + (1,) * (len(dims) - 1 - position))
    return loudness


def different_ones(rng, rows, amount, top, lift):
    ranking = jax.random.permutation(jax.random.fold_in(rng, 1), amount)
    favour = ranking
    for power in range(3):
        favour = favour * favour // amount
    favour = favour * lift // amount
    chance = jax.random.randint(jax.random.fold_in(rng, 2), (rows, amount), 0, 4096) + favour
    sure = jax.random.permutation(jax.random.fold_in(rng, 3), rows)[jnp.arange(amount) % rows]
    chance = jnp.where(jnp.arange(rows)[:, None] == sure[None, :], 1 << 14, chance)
    priority = chance * amount + jnp.arange(amount)
    return lax.top_k(priority.astype(jnp.int32), top)[1].astype(jnp.int32)


def length_profile(number_of, total, limit, lean):
    loads = [(1 << 20) // math.isqrt(standing ** lean) + 1 for standing in range(2, number_of + 1)]
    spare, holding = total - limit - (number_of - 1), [1] * (number_of - 1)
    while spare > 0:
        free = [i for i in range(number_of - 1) if holding[i] < limit]
        pool, remaining = sum([loads[i] for i in free]), spare
        for i in free:
            addition = min(limit - holding[i], max(1, remaining * loads[i] // pool), spare)
            holding[i] = holding[i] + addition
            spare = spare - addition
    return np.array([limit] + holding)


def uneven_parts(rng, count, total, bound, skew):
    if count == 2:
        one = jax.random.randint(rng, (), max(1, total - bound), min(bound, total - 1) + 1)
        return jnp.stack([one, total - one])
    tallies = jnp.asarray(length_profile(count, total, bound, skew), jnp.int32)
    pairs = (count - 1) // 2
    giver, receiver = tallies[1:1 + 2 * pairs:2], tallies[2:2 + 2 * pairs:2]
    slack = jnp.minimum(giver - 1, bound - receiver)
    passed = jax.random.randint(jax.random.fold_in(rng, 1), (pairs,), 0, 1 << 20) % (slack + 1)
    tallies = tallies.at[1:1 + 2 * pairs:2].set(giver - passed).at[2:2 + 2 * pairs:2].set(receiver + passed)
    return tallies[jax.random.permutation(jax.random.fold_in(rng, 2), count)]


def normal_values(key, extent, deviation, limit, pieces=(), kind=jnp.bfloat16):
    result = jax.random.normal(key, extent, jnp.float32) * deviation
    if len(pieces) > 0:
        result = block_scale(key, extent, pieces, -0.22, 0.18) * result
    return jnp.clip(result, min=-limit, max=limit).astype(kind)


def noise_with(stream_key, shape, deviation, bound, split, heavy, kind=jnp.bfloat16):
    result = deviation * jax.random.normal(stream_key, shape, jnp.float32)
    if split:
        result = result * block_scale(stream_key, shape, split, -0.22, 0.18)
    return jnp.clip(spiked(result, jax.random.fold_in(stream_key, 3), *heavy), -bound, bound).astype(kind)


def setup_inputs(seed: int = 0) -> dict:
    key_of = jax.random.split(jax.random.key(seed), 6)
    return {
        "hidden": normal_values(key_of[0], (PATHS, TOK, FF), 1.0, 6.0, ((0, 12), (2, 64))),
        "weights": noise_with(key_of[1], (PATHS, FF, D), FF ** -0.5, 0.125, ((0, 12), (1, 64)), (1, 2, 64, 4.0)),
        "target": normal_values(key_of[2], (PATHS, TOK, D), 1.0, 6.0, ((0, 12), (2, 64))),
        "module": different_ones(key_of[3], PATHS, MODS, 1, 2048),
        "counts": uneven_parts(key_of[4], PATHS, (PATHS + 1) * TOK // 2, TOK, 1).astype(jnp.int32),
    }


def reference(hidden, weights, target, module, counts):
    factor = 1.0 / math.sqrt(TOK)
    module_ids = module[:, 0]
    weight_float = counts.astype(jnp.float32)

    def path_delta(path_index):
        activations = hidden[path_index]
        output = jnp.dot(activations, weights[path_index], preferred_element_type=jnp.float32)
        live_mask = jnp.arange(TOK, dtype=jnp.int32) < counts[path_index]
        error = jnp.where(live_mask[:, None], (output - target[path_index].astype(jnp.float32)) * factor, 0.0).astype(jnp.bfloat16)
        return lax.dot_general(activations, error, (((0,), (0,)), ((), ())), preferred_element_type=jnp.float32).astype(jnp.bfloat16)
    deltas = lax.map(path_delta, jnp.arange(PATHS, dtype=jnp.int32))

    def module_mean(module_index):

        def add_member(carry, member):
            share = jnp.where(module_ids[member] == module_index, weight_float[member], jnp.float32(0.0))
            return (carry + share * deltas[member].astype(jnp.float32), None)
        total, unused = lax.scan(add_member, jnp.zeros((FF, D), jnp.float32), jnp.arange(PATHS, dtype=jnp.int32))
        return total / jnp.sum(jnp.where(module_ids == module_index, weight_float, jnp.float32(0.0)))
    pooled = lax.map(module_mean, jnp.arange(MODS, dtype=jnp.int32))

    def path_update(path_index):
        return pooled[module_ids[path_index]].astype(jnp.bfloat16)
    return lax.map(path_update, jnp.arange(PATHS, dtype=jnp.int32))
```

```python
import functools
import math

import jax
import jax.numpy as jnp
from jax import lax
from jax.experimental import pallas as pl
from jax.experimental.pallas import tpu as pltpu
from jax.sharding import PartitionSpec as P

MESH = pl.DeviceIdType.MESH
BF = jnp.bfloat16
F32 = jnp.float32
LANES = 128


def kernel(X, Y, Z, RC, h_ref, w_ref, t_ref, m_ref, n_ref, o_ref,
           hp, tp, tr, hz, own, sibs, sibr, xs, xr, ys, yr, ez, sel, hc, ea,
           t_sem, h_send, h_recv, sib_send, sib_recv, x_send, x_recv, y_send, y_recv, e_send, e_recv, a_send, a_recv, a_sib):
    z = lax.axis_index("group")
    t = lax.axis_index("tensor")
    x, y, c = t // (2 * Y), (t // 2) % Y, t % 2
    tokens, rows = h_ref.shape
    half = tokens // 2
    other = 1 - c

    def wrap(value, size):
        return lax.rem(value + 2 * size, size)

    def at(px, py, pz, pc):
        return (pz, (px * Y + py) * 2 + pc)

    def copy(src, dst, send, recv, device):
        return pltpu.make_async_remote_copy(
            src_ref=src, dst_ref=dst, send_sem=send, recv_sem=recv, device_id=device, device_id_type=MESH
        )

    sibling = at(x, y, z, other)

    barrier = pltpu.get_barrier_semaphore()

    def greet(device):
        pl.semaphore_signal(barrier, inc=1, device_id=device, device_id_type=MESH)

    greet(sibling)
    for d in range(1, X):
        greet(at(wrap(x + d, X), y, z, c))
    for d in range(1, Y):
        greet(at(x, wrap(y + d, Y), z, c))
    for d in range(1, Z):
        greet(at(x, y, wrap(z + d, Z), c))

    slot = lax.broadcasted_iota(jnp.int32, (tokens, tokens), 0)
    token = lax.broadcasted_iota(jnp.int32, (tokens, tokens), 1)
    order = jnp.where(token == 2 * slot - jnp.where(slot >= half, tokens - 1, 0), 1.0, 0.0).astype(BF)
    hperm = jnp.dot(order, h_ref[...], preferred_element_type=F32)
    tperm = jnp.dot(order, t_ref[...], preferred_element_type=F32).astype(BF)
    twice = jnp.concatenate([tperm, tperm], axis=1)
    hturn = hperm.T.astype(BF)
    for k in range(2):
        hp[k] = hperm[k * half:(k + 1) * half].astype(BF)
        tp[k] = twice[k * half:(k + 1) * half]
        hz[z, k] = hturn[:, k * half:(k + 1) * half]

    pl.semaphore_wait(barrier, 1 + (X - 1) + (Y - 1) + (Z - 1))

    up, down = at(x, y, wrap(z + 1, Z), c), at(x, y, wrap(z - 1, Z), c)
    up_hops, down_hops = Z // 2, Z - 1 - Z // 2

    def hidden_copy(way, hop, k):
        source = wrap(z - (hop - 1), Z) if way == 0 else wrap(z + (hop - 1), Z)
        return copy(hz.at[source, k], hz.at[source, k], h_send.at[way, hop - 1, k], h_recv.at[source, k],
                    up if way == 0 else down)

    def hidden_arrived(way, hop, k):
        source = wrap(z - hop, Z) if way == 0 else wrap(z + hop, Z)
        copy(hz.at[source, k], hz.at[source, k], h_send.at[way, hop - 1, k], h_recv.at[source, k], up).wait_recv()

    def hidden_hop(hop):
        for k in range(2):
            for way, hops in ((0, up_hops), (1, down_hops)):
                if 1 < hop <= hops + 1:
                    hidden_arrived(way, hop - 1, k)
                if hop <= hops:
                    hidden_copy(way, hop, k).start()

    hidden_hop(1)
    target_copy = copy(tp.at[other], tr, t_sem.at[0], t_sem.at[1], sibling)
    target_copy.start()

    def sib_copy(k):
        return copy(sibs.at[k], sibr.at[k], sib_send.at[k], sib_recv.at[k], sibling)

    def partial_step(k, carry):
        to_y = wrap(y + 1 + k, Y)
        columns = jnp.concatenate(
            [w_ref[:, pl.ds(pl.multiple_of((i * Y + to_y) * LANES, LANES), LANES)] for i in range(X)], axis=1
        )
        theirs = jnp.dot(hp[other], columns, preferred_element_type=F32).astype(BF)
        for i in range(X):
            sibs[k, i] = theirs[:, i * LANES:(i + 1) * LANES]
        sib_copy(k).start()
        mine = jnp.dot(hp[c], columns, preferred_element_type=F32)
        for i in range(X):
            own[k, i] = mine[:, i * LANES:(i + 1) * LANES]
        return carry

    lax.fori_loop(0, Y, partial_step, 0)
    hidden_hop(2)

    def x_copy(k, d):
        return copy(xs.at[k, wrap(x + d, X)], xr.at[k, d - 1], x_send.at[k, d - 1], x_recv.at[k, d - 1],
                    at(wrap(x + d, X), y, z, c))

    def x_step(k, carry):
        sib_copy(k).wait_recv()
        for i in range(X):
            value = own[k, i] + sibr[k, i].astype(F32)
            own[k, i] = value
            xs[k, i] = value.astype(BF)
        for d in range(1, X):
            x_copy(k, d).start()
        return carry

    lax.fori_loop(0, Y, x_step, 0)
    hidden_hop(3)

    def y_copy(k):
        return copy(ys.at[k], yr.at[k], y_send.at[k], y_recv.at[k], at(x, wrap(y + 1 + k, Y), z, c))

    def x_sum(k):
        value = own[k, x]
        for d in range(1, X):
            x_copy(k, d).wait_recv()
            value = value + xr[k, d - 1].astype(F32)
        return value

    def y_step(k, carry):
        ys[k] = x_sum(k).astype(BF)
        y_copy(k).start()
        return carry

    stop = (Y - 1) // 3
    lax.fori_loop(0, stop, y_step, 0)
    hidden_hop(4)
    lax.fori_loop(stop, 2 * stop, y_step, 0)
    hidden_hop(5)
    lax.fori_loop(2 * stop, Y - 1, y_step, 0)
    hidden_hop(6)
    total = x_sum(Y - 1)

    def y_sum(k, value):
        y_copy(k).wait_recv()
        return value + yr[k].astype(F32)

    total = lax.fori_loop(0, Y - 1, y_sum, total)

    my_module = m_ref[z]
    weight_sum = jnp.int32(0)
    live = []
    start = [jnp.int32(0), jnp.int32(0)]
    for q in range(Z):
        same = jnp.where(m_ref[q] == my_module, 1, 0)
        weight_sum = weight_sum + same * n_ref[q]
        entry = []
        for k in range(2):
            number = same * lax.div(n_ref[q] + 1 - k, 2)
            entry.append((start[k], number))
            start[k] = start[k] + number
        live.append(entry)
    share = jnp.full((1, LANES), n_ref[z], jnp.int32).astype(F32) / jnp.full((1, LANES), weight_sum, jnp.int32).astype(F32)

    target_copy.wait_recv()
    low = jnp.where(c == 0, tp[c].astype(F32), tr[...].astype(F32))
    high = jnp.where(c == 0, tr[...].astype(F32), tp[c].astype(F32))
    lane = lax.broadcasted_iota(jnp.int32, (half, LANES), 1)
    target = jnp.where(lane < LANES // 2, low, high)
    ez[z] = ((total - target) * (1.0 / math.sqrt(tokens)) * share).astype(BF)

    def e_copy(d):
        return copy(ez.at[z], ez.at[z], e_send.at[d - 1], e_recv.at[z], at(x, y, wrap(z + d, Z), c))

    for d in [k // 2 + 1 if k % 2 == 0 else Z - 1 - k // 2 for k in range(Z - 1)]:
        e_copy(d).start()

    gap = lax.broadcasted_iota(jnp.int32, (RC, half), 0) - lax.broadcasted_iota(jnp.int32, (RC, half), 1)
    column = lax.broadcasted_iota(jnp.int32, (RC, half), 1)
    for k in range(2):
        for q in range(Z):
            first, number = live[q][k]
            sel[k, :, q * half:(q + 1) * half] = jnp.where((gap == first) & (column < number), 1.0, 0.0).astype(BF)

    def e_arrived(d):
        source = wrap(z + d, Z)
        copy(ez.at[source], ez.at[source], e_send.at[0], e_recv.at[source], up).wait_recv()

    for d in range(1, Z):
        e_arrived(d)
    errors = ez[...].reshape(Z * half, LANES)
    ea[x * Y + y, c] = jnp.dot(sel[c], errors, preferred_element_type=F32).astype(BF)

    def block(px, py):
        return wrap(px, X) * Y + wrap(py, Y)

    def a_copy(j, kind):
        if kind == 0:
            device = at(x, wrap(y + 1, Y), z, c)
        elif kind == 1:
            device = at(x, wrap(y - 1, Y), z, c)
        elif kind == 2:
            return copy(ea.at[j, c], ea.at[j, c], a_send.at[j, 2], a_sib.at[j], sibling)
        else:
            device = at(wrap(x + kind - 2, X), y, z, c)
        return copy(ea.at[j, c], ea.at[j, c], a_send.at[j, kind], a_recv.at[j], device)

    y_up, y_down = Y // 2, Y - 1 - Y // 2
    x_kinds = tuple(range(3, 2 + X))

    def spread(phase):
        def visit(j, kinds, arrives=True):
            if phase == 0 and arrives:
                a_copy(j, 0).wait_recv()
            for kind in kinds:
                if phase == 0:
                    a_copy(j, kind).start()
                else:
                    a_copy(j, kind).wait_send()

        visit(block(x, y), (0, 1, 2) + x_kinds, arrives=False)

        @pl.when(c == 0)
        def _():
            for d in range(1, X):
                visit(block(x - d, y), (0, 1, 2))

            def hop_step(i, carry):
                hop, px = i // X + 1, x - i % X
                j = block(px, y - hop)

                @pl.when(hop < y_up)
                def _():
                    visit(j, (0, 2))

                @pl.when(hop == y_up)
                def _():
                    visit(j, (2,))

                j2 = block(px, y + hop)

                @pl.when(hop < y_down)
                def _():
                    visit(j2, (1, 2))

                @pl.when(hop == y_down)
                def _():
                    visit(j2, (2,))

                return carry

            lax.fori_loop(0, X * y_up, hop_step, 0)

        @pl.when(c == 1)
        def _():
            for hop in range(1, y_up + 1):
                visit(block(x, y - hop), ((0,) if hop < y_up else ()) + x_kinds + (2,))
                if hop <= y_down:
                    visit(block(x, y + hop), ((1,) if hop < y_down else ()) + x_kinds + (2,))

            def side_step(i, carry):
                hop, d = i // (X - 1), i % (X - 1) + 1
                visit(block(x - d, y - hop), (2,))

                @pl.when((hop > 0) & (hop <= y_down))
                def _():
                    visit(block(x - d, y + hop), (2,))

                return carry

            lax.fori_loop(0, (y_up + 1) * (X - 1), side_step, 0)

    hidden_hop(7)
    for k in range(2):
        wide = jnp.concatenate([hz[q, k] for q in range(Z)], axis=1)
        hc[k] = lax.dot_general(wide, sel[k], (((1,), (1,)), ((), ())), preferred_element_type=F32).astype(BF)

    spread(0)

    def out_step(i, carry):
        for n in range(2):
            copy(ea.at[2 * i + n, other], ea.at[2 * i + n, other], a_send.at[2 * i + n, 2], a_sib.at[2 * i + n], sibling).wait_recv()
        value = None
        for k in range(2):
            right = jnp.concatenate([ea[2 * i, k], ea[2 * i + 1, k]], axis=1)
            term = jnp.dot(hc[k], right, preferred_element_type=F32)
            value = term if value is None else value + term
        o_ref[:, pl.ds(pl.multiple_of(i * 2 * LANES, 2 * LANES), 2 * LANES)] = value.astype(BF)
        return carry

    lax.fori_loop(0, X * Y // 2, out_step, 0)

    target_copy.wait_send()
    for k in range(2):
        for way, hops in ((0, up_hops), (1, down_hops)):
            for hop in range(1, hops + 1):
                hidden_copy(way, hop, k).wait_send()

    def sent_step(k, carry):
        sib_copy(k).wait_send()
        for d in range(1, X):
            x_copy(k, d).wait_send()
        return carry

    lax.fori_loop(0, Y, sent_step, 0)

    def sent_y(k, carry):
        y_copy(k).wait_send()
        return carry

    lax.fori_loop(0, Y - 1, sent_y, 0)
    for d in range(1, Z):
        e_copy(d).wait_send()
    spread(1)


def call(X, Y, Z, RC, hidden, weights, target, module, counts):
    tokens, rows = hidden.shape
    features = weights.shape[1]
    half = tokens // 2
    vmem = pl.BlockSpec(memory_space=pltpu.VMEM)
    smem = pl.BlockSpec(memory_space=pltpu.SMEM)
    dma = pltpu.SemaphoreType.DMA
    return pl.pallas_call(
        functools.partial(kernel, X, Y, Z, RC),
        out_shape=jax.ShapeDtypeStruct((rows, features), BF),
        in_specs=[vmem, vmem, vmem, smem, smem],
        out_specs=vmem,
        scratch_shapes=[
            pltpu.VMEM((2, half, rows), BF),
            pltpu.VMEM((2, half, LANES), BF),
            pltpu.VMEM((half, LANES), BF),
            pltpu.VMEM((Z, 2, rows, half), BF),
            pltpu.VMEM((Y, X, half, LANES), F32),
            pltpu.VMEM((Y, X, half, LANES), BF),
            pltpu.VMEM((Y, X, half, LANES), BF),
            pltpu.VMEM((Y, X, half, LANES), BF),
            pltpu.VMEM((Y, X - 1, half, LANES), BF),
            pltpu.VMEM((Y - 1, half, LANES), BF),
            pltpu.VMEM((Y - 1, half, LANES), BF),
            pltpu.VMEM((Z, half, LANES), BF),
            pltpu.VMEM((2, RC, Z * half), BF),
            pltpu.VMEM((2, rows, RC), BF),
            pltpu.VMEM((X * Y, 2, RC, LANES), BF),
            dma((2,)),
            dma((2, Z // 2, 2)),
            dma((Z, 2)),
            dma((Y,)),
            dma((Y,)),
            dma((Y, X - 1)),
            dma((Y, X - 1)),
            dma((Y - 1,)),
            dma((Y - 1,)),
            dma((Z - 1,)),
            dma((Z,)),
            dma((X * Y, 2 + X)),
            dma((X * Y,)),
            dma((X * Y,)),
        ],
        compiler_params=pltpu.CompilerParams(collective_id=0, has_side_effects=True, vmem_limit_bytes=56 * 2**20),
        name="step",
    )(hidden, weights, target, module, counts)


def on_device(X, Y, Z, RC, hidden, weights, target, module, counts):
    return call(X, Y, Z, RC, hidden[0], weights[0], target[0], module[:, 0], counts)[None]


def solution(mesh):
    in_specs = (
        P("group", None, "tensor"),
        P("group", "tensor", None),
        P("group", None, "tensor"),
        P(),
        P(),
    )
    return jax.shard_map(
        functools.partial(on_device, 4, 8, 12, 896),
        mesh=mesh, in_specs=in_specs, out_specs=P("group", "tensor", None), check_vma=False,
    )
```

```python
import functools
import math

import jax
import jax.numpy as jnp
from jax import lax
from jax.experimental import pallas as pl
from jax.experimental.pallas import tpu as pltpu
from jax.sharding import PartitionSpec as P

MESH = pl.DeviceIdType.MESH
BF = jnp.bfloat16
F32 = jnp.float32
LANES = 128
SIZES = (160, 192, 224, 448)


def kernel(X, Y, Z, RC, h_hbm, w_hbm, t_hbm, m_ref, n_ref, o_ref,
           h_ref, w_ref, t_ref, hp, tp, tr, hz, own, sibs, sibr, xs, xr, ys, yr, ez, pick, sel, hc, ea,
           load, t_sem, h_send, h_recv, sib_send, sib_recv, x_send, x_recv, y_send, y_recv, e_send, e_recv, a_send, a_recv, a_sib):
    z = lax.axis_index("group")
    t = lax.axis_index("tensor")
    x, y, c = t // (2 * Y), (t // 2) % Y, t % 2
    rows, tokens = h_ref.shape
    half = tokens // 2
    part = half // 2
    other = 1 - c

    def wrap(value, size):
        return lax.rem(value + 2 * size, size)

    def at(px, py, pz, pc):
        return (pz, (px * Y + py) * 2 + pc)

    def copy(src, dst, send, recv, device):
        return pltpu.make_async_remote_copy(
            src_ref=src, dst_ref=dst, send_sem=send, recv_sem=recv, device_id=device, device_id_type=MESH
        )

    sibling = at(x, y, z, other)
    loads = [
        pltpu.make_async_copy(source, target, load.at[i])
        for i, (source, target) in enumerate(((h_hbm, h_ref), (t_hbm, t_ref), (w_hbm, w_ref)))
    ]
    for item in loads:
        item.start()

    barrier = pltpu.get_barrier_semaphore()

    def greet(device):
        pl.semaphore_signal(barrier, inc=1, device_id=device, device_id_type=MESH)

    greet(sibling)
    for d in range(1, X):
        greet(at(wrap(x + d, X), y, z, c))
    for d in range(1, Y):
        greet(at(x, wrap(y + d, Y), z, c))
    for d in range(1, Z):
        greet(at(x, y, wrap(z + d, Z), c))

    slot = lax.broadcasted_iota(jnp.int32, (tokens, tokens), 0)
    token = lax.broadcasted_iota(jnp.int32, (tokens, tokens), 1)
    quarter = slot // part
    order = jnp.where(token == 4 * (slot % part) + 2 * (quarter % 2) + quarter // 2, 1.0, 0.0).astype(BF)
    loads[0].wait()
    loads[1].wait()
    by_last = (((1,), (1,)), ((), ()))
    hperm = lax.dot_general(order, h_ref[...], by_last, preferred_element_type=F32)
    hturn = lax.dot_general(h_ref[...], order, by_last, preferred_element_type=F32)
    tperm = lax.dot_general(order, t_ref[...], by_last, preferred_element_type=F32).astype(BF)
    twice = jnp.concatenate([tperm, tperm], axis=1)
    for k in range(2):
        hp[k] = hperm[k * half:(k + 1) * half].astype(BF)
        tp[k] = twice[k * half:(k + 1) * half]
        hz[z, k] = hturn[:, k * half:(k + 1) * half].astype(BF)

    pl.semaphore_wait(barrier, 1 + (X - 1) + (Y - 1) + (Z - 1))

    up, down = at(x, y, wrap(z + 1, Z), c), at(x, y, wrap(z - 1, Z), c)
    up_hops, down_hops = Z // 2, Z - 1 - Z // 2

    def hidden_copy(way, hop, k):
        source = wrap(z - (hop - 1), Z) if way == 0 else wrap(z + (hop - 1), Z)
        return copy(hz.at[source, k], hz.at[source, k], h_send.at[way, hop - 1, k], h_recv.at[source, k],
                    up if way == 0 else down)

    def hidden_arrived(way, hop, k):
        source = wrap(z - hop, Z) if way == 0 else wrap(z + hop, Z)
        copy(hz.at[source, k], hz.at[source, k], h_send.at[way, hop - 1, k], h_recv.at[source, k], up).wait_recv()

    def hidden_hop(hop):
        for k in range(2):
            for way, hops in ((0, up_hops), (1, down_hops)):
                if 1 < hop <= hops + 1:
                    hidden_arrived(way, hop - 1, k)
                if hop <= hops:
                    hidden_copy(way, hop, k).start()

    hidden_hop(1)
    target_copy = copy(tp.at[other], tr, t_sem.at[0], t_sem.at[1], sibling)
    target_copy.start()

    def sib_copy(k):
        return copy(sibs.at[k], sibr.at[k], sib_send.at[k], sib_recv.at[k], sibling)

    def partial_step(k, carry):
        to_y = wrap(y + 1 + k, Y)
        columns = jnp.concatenate(
            [w_ref[:, pl.ds(pl.multiple_of((i * Y + to_y) * LANES, LANES), LANES)] for i in range(X)], axis=1
        )
        theirs = jnp.dot(hp[other], columns, preferred_element_type=F32).astype(BF)
        for i in range(X):
            sibs[k, i] = theirs[:, i * LANES:(i + 1) * LANES]
        sib_copy(k).start()
        mine = jnp.dot(hp[c], columns, preferred_element_type=F32)
        for i in range(X):
            own[k, i] = mine[:, i * LANES:(i + 1) * LANES]
        return carry

    loads[2].wait()
    lax.fori_loop(0, Y, partial_step, 0)

    def x_copy(p, k, d):
        return copy(xs.at[p, k, wrap(x + d, X)], xr.at[p, k, d - 1], x_send.at[p, k, d - 1], x_recv.at[p, k, d - 1],
                    at(wrap(x + d, X), y, z, c))

    def x_step(k, carry):
        sib_copy(k).wait_recv()
        for i in range(X):
            value = own[k, i] + sibr[k, i].astype(F32)
            own[k, i] = value
            for p in range(2):
                xs[p, k, i] = value[p * part:(p + 1) * part].astype(BF)
        for d in range(1, X):
            x_copy(0, k, d).start()
        return carry

    lax.fori_loop(0, Y, x_step, 0)

    def x_second(k, carry):
        for d in range(1, X):
            x_copy(1, k, d).start()
        return carry

    lax.fori_loop(0, Y, x_second, 0)
    hidden_hop(2)

    my_module = m_ref[z]
    weight_sum = jnp.int32(0)
    live = []
    start = [jnp.int32(0)] * 4
    for q in range(Z):
        same = jnp.where(m_ref[q] == my_module, 1, 0)
        weight_sum = weight_sum + same * n_ref[q]
        entry = []
        for k in range(4):
            number = same * lax.div(n_ref[q] + 3 - k, 4)
            entry.append((start[k], number))
            start[k] = start[k] + number
        live.append(entry)
    share = jnp.full((1, LANES), n_ref[z], jnp.int32).astype(F32) / jnp.full((1, LANES), weight_sum, jnp.int32).astype(F32)


    row = lax.broadcasted_iota(jnp.int32, (RC, LANES), 0)
    lane = lax.broadcasted_iota(jnp.int32, (RC, LANES), 1)
    inner = lane % part
    gap = row - inner
    upper = lane >= part
    for k in range(2):
        for p in range(2):
            here = upper if p == 1 else jnp.logical_not(upper)
            for q in range(Z):
                first, number = live[q][2 * p + k]
                sel[k, p * RC:(p + 1) * RC, q * half:(q + 1) * half] = jnp.where(
                    (gap == first) & (inner < number) & here, 1.0, 0.0
                ).astype(BF)
    for p in range(2):
        for q in range(0, Z, 2):
            firsts, numbers = [], []
            for n in range(2):
                first, number = (jnp.where(c == 0, a, b) for a, b in zip(live[q + n][2 * p], live[q + n][2 * p + 1]))
                firsts.append(first)
                numbers.append(number)
            first = jnp.where(upper, firsts[1], firsts[0])
            number = jnp.where(upper, numbers[1], numbers[0])
            pick[p, :, q * part:(q + 2) * part] = jnp.where((gap == first) & (inner < number), 1.0, 0.0).astype(BF)

    def y_copy(p, k):
        return copy(ys.at[p, k], yr.at[p, k], y_send.at[p, k], y_recv.at[p, k], at(x, wrap(y + 1 + k, Y), z, c))

    def x_sum(p, k):
        value = own[k, x, p * part:(p + 1) * part]
        for d in range(1, X):
            x_copy(p, k, d).wait_recv()
            value = value + xr[p, k, d - 1].astype(F32)
        return value

    def y_step(p, k, carry):
        ys[p, k] = x_sum(p, k).astype(BF)
        y_copy(p, k).start()
        return carry

    def e_copy(p, d):
        return copy(ez.at[p, z], ez.at[p, z], e_send.at[p, d - 1], e_recv.at[p, z], at(x, y, wrap(z + d, Z), c))

    def error_part(p):
        def y_sum(k, value):
            y_copy(p, k).wait_recv()
            return value + yr[p, k].astype(F32)

        total = lax.fori_loop(0, Y - 1, y_sum, x_sum(p, Y - 1))
        mine, theirs = (ref[p * part:(p + 1) * part].astype(F32) for ref in (tp.at[c], tr))
        low = jnp.where(c == 0, mine, theirs)
        high = jnp.where(c == 0, theirs, mine)
        lane = lax.broadcasted_iota(jnp.int32, (part, LANES), 1)
        target = jnp.where(lane < LANES // 2, low, high)
        ez[p, z] = ((total - target) * (1.0 / math.sqrt(tokens)) * share).astype(BF)
        for d in [k // 2 + 1 if k % 2 == 0 else Z - 1 - k // 2 for k in range(Z - 1)]:
            e_copy(p, d).start()

    middle = Y // 2
    lax.fori_loop(0, Y - 1, functools.partial(y_step, 0), 0)
    lax.fori_loop(0, middle, functools.partial(y_step, 1), 0)
    target_copy.wait_recv()
    error_part(0)
    hidden_hop(3)
    lax.fori_loop(middle, Y - 1, functools.partial(y_step, 1), 0)
    error_part(1)

    def block(px, py):
        return wrap(px, X) * Y + wrap(py, Y)

    def a_copy(p, j, kind):
        if kind == 2:
            return copy(ea.at[j, c, p], ea.at[j, c, p], a_send.at[p, j, 2], a_sib.at[p, j], sibling)
        if kind < 2:
            device = at(x, wrap(y + 1 - 2 * kind, Y), z, c)
        else:
            device = at(wrap(x + kind - 2, X), y, z, c)
        return copy(ea.at[j, c, p], ea.at[j, c, p], a_send.at[p, j, kind], a_recv.at[p, j], device)

    x_kinds = tuple(range(3, 2 + X))
    rounds = Y // 2

    def up_limit(px):
        return rounds - lax.rem(wrap(px, X), 2)

    def keep_hidden():
        kept = []
        for k in range(2):
            wide = jnp.concatenate([hz[q, k] for q in range(Z)], axis=1)
            kept.append(lax.dot_general(wide, sel[k], by_last, preferred_element_type=F32).astype(BF))
        hc[...] = jnp.concatenate(kept, axis=1)

    def keep_errors(p):
        for d in range(1, Z):
            source = wrap(z + d, Z)
            copy(ez.at[p, source], ez.at[p, source], e_send.at[p, 0], e_recv.at[p, source], up).wait_recv()
        errors = ez[p].reshape(Z * part, LANES)
        ea[x * Y + y, c, p] = jnp.dot(pick[p], errors, preferred_element_type=F32).astype(BF)

    def spread(phase):
        def act(p, j, kinds):
            for kind in kinds:
                if phase == 0:
                    a_copy(p, j, kind).start()
                else:
                    a_copy(p, j, kind).wait_send()

        def arrived(p, j):
            if phase == 0:
                a_copy(p, j, 0).wait_recv()

        def relay(p, px, py, hop, way, kinds):
            limit = up_limit(px) if way == 0 else Y - 1 - up_limit(px)
            j = block(px, py)

            @pl.when(hop <= limit)
            def _():
                arrived(p, j)

                @pl.when(hop < limit)
                def _():
                    act(p, j, (way,))

                act(p, j, kinds)

        def origin(p):
            if phase == 0:
                keep_errors(p)
            act(p, block(x, y), (0, 1) + x_kinds + (2,))

        def first(p):
            @pl.when(c == 0)
            def _():
                for d in range(1, X):
                    arrived(p, block(x - d, y))
                    act(p, block(x - d, y), (0, 1, 2))

            @pl.when(c == 1)
            def _():
                relay(p, x, y - 1, 1, 0, x_kinds + (2,))
                relay(p, x, y + 1, 1, 1, x_kinds + (2,))

        def along_y(p, hop):
            def hop_step(i, carry):
                relay(p, x - i, y - hop, hop, 0, (2,))
                relay(p, x - i, y + hop, hop, 1, (2,))
                return carry

            lax.fori_loop(0, X, hop_step, 0)

        def along_x(p, hop):
            def side_step(d, carry):
                j = block(x - d, y)
                if hop == 0:
                    arrived(p, j)
                    act(p, j, (2,))
                else:
                    for way, sign in ((0, -1), (1, 1)):
                        limit = up_limit(x - d) if way == 0 else Y - 1 - up_limit(x - d)
                        j = block(x - d, y + sign * hop)

                        @pl.when(hop <= limit)
                        def _(j=j):
                            arrived(p, j)
                            act(p, j, (2,))

                return carry

            lax.fori_loop(1, X, side_step, 0)

        origin(0)
        first(0)
        origin(1)
        if phase == 0:
            hidden_hop(4)
        first(1)
        for hop in range(1, rounds + 1):
            for p in range(2):
                @pl.when(c == 0)
                def _(p=p, hop=hop):
                    along_y(p, hop)

                @pl.when(c == 1)
                def _(p=p, hop=hop):
                    if hop < rounds:
                        relay(p, x, y - hop - 1, hop + 1, 0, x_kinds + (2,))
                        relay(p, x, y + hop + 1, hop + 1, 1, x_kinds + (2,))
                    along_x(p, hop - 1)
                    if hop == rounds:
                        along_x(p, hop)

            if phase == 0 and hop < rounds:
                hidden_hop(hop + 4)
                if hop == rounds - 1:
                    keep_hidden()

    spread(0)

    def out_step(i, carry):
        for n in range(2):
            j = 2 * i + n
            for p in range(2):
                copy(ea.at[j, other, p], ea.at[j, other, p], a_send.at[p, j, 2], a_sib.at[p, j], sibling).wait_recv()
        right = jnp.concatenate([ea[2 * i + n].reshape(4 * RC, LANES) for n in range(2)], axis=1)
        value = jnp.dot(hc[...], right, preferred_element_type=F32)
        o_ref[:, pl.ds(pl.multiple_of(i * 2 * LANES, 2 * LANES), 2 * LANES)] = value.astype(BF)
        return carry

    lax.fori_loop(0, X * Y // 2, out_step, 0)

    target_copy.wait_send()
    for k in range(2):
        for way, hops in ((0, up_hops), (1, down_hops)):
            for hop in range(1, hops + 1):
                hidden_copy(way, hop, k).wait_send()

    def sent_step(k, carry):
        sib_copy(k).wait_send()
        for p in range(2):
            for d in range(1, X):
                x_copy(p, k, d).wait_send()
        return carry

    lax.fori_loop(0, Y, sent_step, 0)

    def sent_y(k, carry):
        for p in range(2):
            y_copy(p, k).wait_send()
        return carry

    lax.fori_loop(0, Y - 1, sent_y, 0)
    for p in range(2):
        for d in range(1, Z):
            e_copy(p, d).wait_send()
    spread(1)


def call(X, Y, Z, RC, number, hidden, weights, target, module, counts):
    rows, tokens = hidden.shape
    features = weights.shape[1]
    half = tokens // 2
    part = half // 2
    hbm = pl.BlockSpec(memory_space=pl.ANY)
    smem = pl.BlockSpec(memory_space=pltpu.SMEM)
    dma = pltpu.SemaphoreType.DMA
    scratch = [
        pltpu.VMEM(hidden.shape, BF),
        pltpu.VMEM(weights.shape, BF),
        pltpu.VMEM(target.shape, BF),
        pltpu.VMEM((2, half, rows), BF),
        pltpu.VMEM((2, half, LANES), BF),
        pltpu.VMEM((half, LANES), BF),
        pltpu.VMEM((Z, 2, rows, half), BF),
        pltpu.VMEM((Y, X, half, LANES), F32),
        pltpu.VMEM((Y, X, half, LANES), BF),
        pltpu.VMEM((Y, X, half, LANES), BF),
        pltpu.VMEM((2, Y, X, part, LANES), BF),
        pltpu.VMEM((2, Y, X - 1, part, LANES), BF),
        pltpu.VMEM((2, Y - 1, part, LANES), BF),
        pltpu.VMEM((2, Y - 1, part, LANES), BF),
        pltpu.VMEM((2, Z, part, LANES), BF),
        pltpu.VMEM((2, RC, Z * part), BF),
        pltpu.VMEM((2, 2 * RC, Z * half), BF),
        pltpu.VMEM((rows, 4 * RC), BF),
        pltpu.VMEM((X * Y, 2, 2, RC, LANES), BF),
        dma((3,)),
        dma((2,)),
        dma((2, Z // 2, 2)),
        dma((Z, 2)),
        dma((Y,)),
        dma((Y,)),
        dma((2, Y, X - 1)),
        dma((2, Y, X - 1)),
        dma((2, Y - 1)),
        dma((2, Y - 1)),
        dma((2, Z - 1)),
        dma((2, Z)),
        dma((2, X * Y, 2 + X)),
        dma((2, X * Y)),
        dma((2, X * Y)),
    ]
    return pl.pallas_call(
        functools.partial(kernel, X, Y, Z, RC),
        out_shape=jax.ShapeDtypeStruct((rows, features), BF),
        in_specs=[hbm, hbm, hbm, smem, smem],
        out_specs=pl.BlockSpec(memory_space=pltpu.VMEM),
        scratch_shapes=scratch,
        compiler_params=pltpu.CompilerParams(
            collective_id=number, has_side_effects=True, vmem_limit_bytes=(18 + RC // 20) * 2**20
        ),
        name=f"step{RC}",
    )(hidden, weights, target, module, counts)


def on_device(X, Y, Z, sizes, hidden, weights, target, module, counts):
    modules, tokens = module[:, 0], hidden.shape[1]
    same = modules[:, None] == modules[None, :]
    most = jnp.max(jnp.sum(jnp.where(same, (counts[None, :] + 3) // 4, 0), axis=1))
    which = jnp.sum(jnp.where(most > jnp.array(sizes[:-1], jnp.int32), 1, 0))
    branches = [functools.partial(call, X, Y, Z, size, i) for i, size in enumerate(sizes)]
    operands = (hidden[0].T, weights[0], target[0].T, modules, counts)
    if len(sizes) == 1:
        return branches[0](*operands)[None]
    return lax.switch(which, branches, *operands)[None]


def solution(mesh):
    in_specs = (
        P("group", None, "tensor"),
        P("group", "tensor", None),
        P("group", None, "tensor"),
        P(),
        P(),
    )
    return jax.shard_map(
        functools.partial(on_device, 4, 8, 12, SIZES),
        mesh=mesh, in_specs=in_specs, out_specs=P("group", "tensor", None), check_vma=False,
    )
```

```python
import functools
import math

import jax
import jax.numpy as jnp
from jax import lax
from jax.experimental import pallas as pl
from jax.experimental.pallas import tpu as pltpu
from jax.sharding import PartitionSpec as P

MESH = pl.DeviceIdType.MESH
BF = jnp.bfloat16
F32 = jnp.float32
LANES = 128
SIZES = (160, 192, 224, 448)


def kernel(X, Y, Z, RC, h_hbm, w_hbm, t_hbm, m_ref, n_ref, o_ref,
           h_ref, w_ref, t_ref, hp, tp, tr, hz, own, sibs, sibr, xs, xr, ys, yr, ez, pick, sel, hc, ea,
           load, t_sem, h_send, h_recv, sib_send, sib_recv, x_send, x_recv, y_send, y_recv, e_send, e_recv, a_send, a_recv, a_x, a_sib):
    z = lax.axis_index("group")
    t = lax.axis_index("tensor")
    x, y, c = t // (2 * Y), (t // 2) % Y, t % 2
    rows, tokens = h_ref.shape
    half = tokens // 2
    part = half // 2
    other = 1 - c

    def wrap(value, size):
        return lax.rem(value + 2 * size, size)

    def at(px, py, pz, pc):
        return (pz, (px * Y + py) * 2 + pc)

    def copy(src, dst, send, recv, device):
        return pltpu.make_async_remote_copy(
            src_ref=src, dst_ref=dst, send_sem=send, recv_sem=recv, device_id=device, device_id_type=MESH
        )

    sibling = at(x, y, z, other)
    loads = [
        pltpu.make_async_copy(source, target, load.at[i])
        for i, (source, target) in enumerate(((h_hbm, h_ref), (t_hbm, t_ref), (w_hbm, w_ref)))
    ]
    for item in loads:
        item.start()

    barrier = pltpu.get_barrier_semaphore()

    def greet(device):
        pl.semaphore_signal(barrier, inc=1, device_id=device, device_id_type=MESH)

    greet(sibling)
    for d in range(1, X):
        greet(at(wrap(x + d, X), y, z, c))
    for d in range(1, Y):
        greet(at(x, wrap(y + d, Y), z, c))
    for d in range(1, Z):
        greet(at(x, y, wrap(z + d, Z), c))

    slot = lax.broadcasted_iota(jnp.int32, (tokens, tokens), 0)
    token = lax.broadcasted_iota(jnp.int32, (tokens, tokens), 1)
    quarter = slot // part
    order = jnp.where(token == 4 * (slot % part) + 2 * (quarter % 2) + quarter // 2, 1.0, 0.0).astype(BF)
    loads[0].wait()
    loads[1].wait()
    by_last = (((1,), (1,)), ((), ()))
    hperm = lax.dot_general(order, h_ref[...], by_last, preferred_element_type=F32)
    hturn = lax.dot_general(h_ref[...], order, by_last, preferred_element_type=F32)
    tperm = lax.dot_general(order, t_ref[...], by_last, preferred_element_type=F32).astype(BF)
    twice = jnp.concatenate([tperm, tperm], axis=1)
    for k in range(2):
        hp[k] = hperm[k * half:(k + 1) * half].astype(BF)
        tp[k] = twice[k * half:(k + 1) * half]
        hz[z, k] = hturn[:, k * half:(k + 1) * half].astype(BF)

    pl.semaphore_wait(barrier, 1 + (X - 1) + (Y - 1) + (Z - 1))

    up, down = at(x, y, wrap(z + 1, Z), c), at(x, y, wrap(z - 1, Z), c)
    up_hops, down_hops = Z // 2, Z - 1 - Z // 2

    def hidden_copy(way, hop):
        source = wrap(z - (hop - 1), Z) if way == 0 else wrap(z + (hop - 1), Z)
        return copy(hz.at[source], hz.at[source], h_send, h_recv.at[source], up if way == 0 else down)

    def hidden_hop(hop):
        for way, hops in ((0, up_hops), (1, down_hops)):
            if 1 < hop <= hops + 1:
                source = wrap(z - (hop - 1), Z) if way == 0 else wrap(z + (hop - 1), Z)
                copy(hz.at[source], hz.at[source], h_send, h_recv.at[source], up).wait_recv()
            if hop <= hops:
                hidden_copy(way, hop).start()

    hidden_hop(1)
    target_copy = copy(tp.at[other], tr, t_sem.at[0], t_sem.at[1], sibling)
    target_copy.start()

    def sib_copy(k):
        return copy(sibs.at[k], sibr.at[k], sib_send, sib_recv.at[k], sibling)

    def partial_step(k, carry):
        to_y = wrap(y + 1 + k, Y)
        columns = jnp.concatenate(
            [w_ref[:, pl.ds(pl.multiple_of((i * Y + to_y) * LANES, LANES), LANES)] for i in range(X)], axis=1
        )
        theirs = jnp.dot(hp[other], columns, preferred_element_type=F32).astype(BF)
        for i in range(X):
            sibs[k, i] = theirs[:, i * LANES:(i + 1) * LANES]
        sib_copy(k).start()
        mine = jnp.dot(hp[c], columns, preferred_element_type=F32)
        for i in range(X):
            own[k, i] = mine[:, i * LANES:(i + 1) * LANES]
        return carry

    loads[2].wait()
    lax.fori_loop(0, 2, partial_step, 0)

    def x_copy(p, m, d):
        pair = pl.ds(2 * m, 2)
        return copy(xs.at[p, pair, wrap(x + d, X)], xr.at[p, pair, d - 1], x_send, x_recv.at[p, m],
                    at(wrap(x + d, X), y, z, c))

    def x_step(m, carry):
        for n in range(2):
            k = 2 * m + n
            sib_copy(k).wait_recv()
            for i in range(X):
                value = own[k, i] + sibr[k, i].astype(F32)
                own[k, i] = value
                for p in range(2):
                    xs[p, k, i] = value[p * part:(p + 1) * part].astype(BF)
        for d in range(1, X):
            x_copy(0, m, d).start()
        return carry

    def pair_step(m, carry):
        for n in range(2):
            partial_step(2 * m + 2 + n, carry)
        return x_step(m, carry)

    lax.fori_loop(0, Y // 2 - 1, pair_step, 0)
    x_step(Y // 2 - 1, 0)

    def x_second(m, carry):
        for d in range(1, X):
            x_copy(1, m, d).start()
        return carry

    lax.fori_loop(0, Y // 2, x_second, 0)
    hidden_hop(2)

    my_module = m_ref[z]
    weight_sum = jnp.int32(0)
    live = []
    start = [jnp.int32(0)] * 4
    for q in range(Z):
        same = jnp.where(m_ref[q] == my_module, 1, 0)
        weight_sum = weight_sum + same * n_ref[q]
        entry = []
        for k in range(4):
            number = same * lax.div(n_ref[q] + 3 - k, 4)
            entry.append((start[k], number))
            start[k] = start[k] + number
        live.append(entry)
    share = jnp.full((1, LANES), n_ref[z], jnp.int32).astype(F32) / jnp.full((1, LANES), weight_sum, jnp.int32).astype(F32)


    row = lax.broadcasted_iota(jnp.int32, (RC, LANES), 0)
    lane = lax.broadcasted_iota(jnp.int32, (RC, LANES), 1)
    inner = lane % part
    gap = row - inner
    upper = lane >= part
    for k in range(2):
        for p in range(2):
            here = upper if p == 1 else jnp.logical_not(upper)
            for q in range(Z):
                first, number = live[q][2 * p + k]
                sel[k, p * RC:(p + 1) * RC, q * half:(q + 1) * half] = jnp.where(
                    (gap == first) & (inner < number) & here, 1.0, 0.0
                ).astype(BF)
    for p in range(2):
        for q in range(0, Z, 2):
            firsts, numbers = [], []
            for n in range(2):
                first, number = (jnp.where(c == 0, a, b) for a, b in zip(live[q + n][2 * p], live[q + n][2 * p + 1]))
                firsts.append(first)
                numbers.append(number)
            first = jnp.where(upper, firsts[1], firsts[0])
            number = jnp.where(upper, numbers[1], numbers[0])
            pick[p, :, q * part:(q + 2) * part] = jnp.where((gap == first) & (inner < number), 1.0, 0.0).astype(BF)

    def y_copy(p, k):
        return copy(ys.at[p, k], yr.at[p, k], y_send, y_recv.at[p], at(x, wrap(y + 1 + k, Y), z, c))

    def x_arrived(p, m):
        pair = xr.at[p, pl.ds(2 * m, 2)]
        copy(pair, pair, x_send, x_recv.at[p, m], sibling).wait_recv()

    def x_sum(p, k):
        value = own[k, x, p * part:(p + 1) * part]
        for d in range(1, X):
            value = value + xr[p, k, d - 1].astype(F32)
        return value

    def y_start(p, k):
        ys[p, k] = x_sum(p, k).astype(BF)
        y_copy(p, k).start()

    def y_step(p, m, carry):
        x_arrived(p, m)
        for n in range(2):
            y_start(p, 2 * m + n)
        return carry

    def y_last(p):
        x_arrived(p, Y // 2 - 1)
        y_start(p, Y - 2)

    def e_copy(p, d):
        return copy(ez.at[p, z], ez.at[p, z], e_send, e_recv.at[p], at(x, y, wrap(z + d, Z), c))

    def error_part(p):
        total = x_sum(p, Y - 1)
        copy(yr.at[p], yr.at[p], y_send, y_recv.at[p], sibling).wait_recv()
        for k in range(Y - 1):
            total = total + yr[p, k].astype(F32)
        mine, theirs = (ref[p * part:(p + 1) * part].astype(F32) for ref in (tp.at[c], tr))
        low = jnp.where(c == 0, mine, theirs)
        high = jnp.where(c == 0, theirs, mine)
        lane = lax.broadcasted_iota(jnp.int32, (part, LANES), 1)
        target = jnp.where(lane < LANES // 2, low, high)
        ez[p, z] = ((total - target) * (1.0 / math.sqrt(tokens)) * share).astype(BF)
        for d in [k // 2 + 1 if k % 2 == 0 else Z - 1 - k // 2 for k in range(Z - 1)]:
            e_copy(p, d).start()

    lax.fori_loop(0, Y // 2 - 1, functools.partial(y_step, 0), 0)
    hidden_hop(3)
    y_last(0)
    lax.fori_loop(0, Y // 2 - 2, functools.partial(y_step, 1), 0)
    target_copy.wait_recv()
    error_part(0)
    lax.fori_loop(Y // 2 - 2, Y // 2 - 1, functools.partial(y_step, 1), 0)
    y_last(1)
    error_part(1)
    hidden_hop(4)

    rounds = Y // 2
    everyone = pl.ds(0, X)

    def place(hop, way):
        return min(2 * hop - 1 + way, Y - 1)

    def ring(hop):
        if hop == 0:
            return pl.ds(0, 1)
        return pl.ds(2 * hop - 1, 2) if hop < rounds else pl.ds(Y - 1, 1)

    def ways(p, core, hop):
        if hop > rounds:
            return ()
        return (0, 1) if hop < rounds else ((p + core) % 2,)

    def along_y(p, core, hop):
        columns = everyone if core == 0 else pl.ds(0, 1)
        for way in ways(p, core, hop):
            before = 0 if hop == 1 else place(hop - 1, way)
            after = place(hop, way)
            copy(ea.at[before, columns, core, p], ea.at[after, columns, core, p], a_send.at[p, 0], a_recv.at[p, after],
                 at(x, wrap(y + 1 - 2 * way, Y), z, c)).start()

    def y_arrived(p, core, hop):
        columns = everyone if core == 0 else pl.ds(0, 1)
        for way in ways(p, core, hop):
            block = ea.at[place(hop, way), columns, core, p]
            copy(block, block, a_send.at[p, 0], a_recv.at[p, place(hop, way)], sibling).wait_recv()

    def along_x(p, core, hop):
        for d in range(1, X):
            copy(ea.at[ring(hop), 0, core, p], ea.at[ring(hop), d, core, p], a_send.at[p, 2], a_x.at[p, hop],
                 at(wrap(x + d, X), y, z, c)).start()

    def x_blocks_arrived(p, core, hop):
        blocks = ea.at[ring(hop), pl.ds(1, X - 1), core, p]
        copy(blocks, blocks, a_send.at[p, 2], a_x.at[p, hop], sibling).wait_recv()

    def hand_over(p, core, hop):
        blocks = ea.at[ring(hop), everyone, core, p]
        copy(blocks, blocks, a_send.at[p, 1], a_sib.at[p, hop], sibling).start()

    def keep_hidden():
        kept = []
        for k in range(2):
            wide = jnp.concatenate([hz[q, k] for q in range(Z)], axis=1)
            kept.append(lax.dot_general(wide, sel[k], by_last, preferred_element_type=F32).astype(BF))
        hc[...] = jnp.concatenate(kept, axis=1)

    def keep_errors(p):
        others = ez.at[p, pl.ds(0, Z - 1)]
        copy(others, others, e_send, e_recv.at[p], sibling).wait_recv()
        errors = ez[p].reshape(Z * part, LANES)
        ea[0, 0, c, p] = jnp.dot(pick[p], errors, preferred_element_type=F32).astype(BF)

    def origin(p):
        keep_errors(p)

        @pl.when(c == 0)
        def _():
            along_x(p, 0, 0)

        @pl.when(c == 1)
        def _():
            along_y(p, 1, 1)
            along_x(p, 1, 0)

    def first(p):
        @pl.when(c == 0)
        def _():
            x_blocks_arrived(p, 0, 0)
            along_y(p, 0, 1)
            hand_over(p, 0, 0)

        @pl.when(c == 1)
        def _():
            y_arrived(p, 1, 1)
            along_y(p, 1, 2)
            along_x(p, 1, 1)

    def further(p, hop):
        @pl.when(c == 0)
        def _():
            y_arrived(p, 0, hop)
            along_y(p, 0, hop + 1)
            hand_over(p, 0, hop)

        @pl.when(c == 1)
        def _():
            if hop < rounds:
                y_arrived(p, 1, hop + 1)
                along_y(p, 1, hop + 2)
                along_x(p, 1, hop + 1)
            x_blocks_arrived(p, 1, hop - 1)
            hand_over(p, 1, hop - 1)
            if hop == rounds:
                x_blocks_arrived(p, 1, hop)
                hand_over(p, 1, hop)

    origin(0)
    first(0)
    origin(1)
    hidden_hop(5)
    first(1)
    def out_step(n, carry):
        i, d = n // (X // 2), n % (X // 2) * 2
        right = jnp.concatenate([ea[i, d + m].reshape(4 * RC, LANES) for m in range(2)], axis=1)
        value = jnp.dot(hc[...], right, preferred_element_type=F32).astype(BF)
        py = wrap(y + (i + 1) // 2 * (1 - 2 * (i % 2)), Y)
        for m in range(2):
            j = wrap(x - d - m, X) * Y + py
            o_ref[:, pl.ds(pl.multiple_of(j * LANES, LANES), LANES)] = value[:, m * LANES:(m + 1) * LANES]
        return carry

    def out(hop):
        for p in range(2):
            blocks = ea.at[ring(hop), everyone, other, p]
            copy(blocks, blocks, a_send.at[p, 1], a_sib.at[p, hop], sibling).wait_recv()
        low = max(2 * hop - 1, 0)
        lax.fori_loop(low * (X // 2), min(2 * hop + 1, Y) * (X // 2), out_step, 0)

    for hop in range(1, rounds + 1):
        for p in range(2):
            further(p, hop)
        if hop <= 2:
            hidden_hop(hop + 5)
        if hop == 2:
            keep_hidden()
        if hop == rounds - 1:
            for done in range(rounds - 1):
                out(done)
    for done in range(rounds - 1, rounds + 1):
        out(done)

    def sent(bytes_of, semaphore):
        copy(bytes_of, bytes_of, semaphore, t_sem.at[1], sibling).wait_send()

    sent(tr, t_sem.at[0])
    sent(hz.at[pl.ds(0, Z - 1)], h_send)
    sent(sibs, sib_send)
    sent(xr, x_send)
    sent(ys, y_send)
    sent(ez.at[:, pl.ds(0, Z - 1)], e_send)
    for p in range(2):
        sent(ea.at[:, :, c, p], a_send.at[p, 1])

        @pl.when(c == 0)
        def _(p=p):
            sent(ea.at[pl.ds(0, Y - 1), :, 0, p], a_send.at[p, 0])
            sent(ea.at[0, pl.ds(0, X - 1), 0, p], a_send.at[p, 2])

        @pl.when(c == 1)
        def _(p=p):
            sent(ea.at[pl.ds(0, Y - 1), 0, 1, p], a_send.at[p, 0])
            sent(ea.at[:, pl.ds(0, X - 1), 1, p], a_send.at[p, 2])


def call(X, Y, Z, RC, number, hidden, weights, target, module, counts):
    rows, tokens = hidden.shape
    features = weights.shape[1]
    half = tokens // 2
    part = half // 2
    hbm = pl.BlockSpec(memory_space=pl.ANY)
    smem = pl.BlockSpec(memory_space=pltpu.SMEM)
    dma = pltpu.SemaphoreType.DMA
    scratch = [
        pltpu.VMEM(hidden.shape, BF),
        pltpu.VMEM(weights.shape, BF),
        pltpu.VMEM(target.shape, BF),
        pltpu.VMEM((2, half, rows), BF),
        pltpu.VMEM((2, half, LANES), BF),
        pltpu.VMEM((half, LANES), BF),
        pltpu.VMEM((Z, 2, rows, half), BF),
        pltpu.VMEM((Y, X, half, LANES), F32),
        pltpu.VMEM((Y, X, half, LANES), BF),
        pltpu.VMEM((Y, X, half, LANES), BF),
        pltpu.VMEM((2, Y, X, part, LANES), BF),
        pltpu.VMEM((2, Y, X - 1, part, LANES), BF),
        pltpu.VMEM((2, Y - 1, part, LANES), BF),
        pltpu.VMEM((2, Y - 1, part, LANES), BF),
        pltpu.VMEM((2, Z, part, LANES), BF),
        pltpu.VMEM((2, RC, Z * part), BF),
        pltpu.VMEM((2, 2 * RC, Z * half), BF),
        pltpu.VMEM((rows, 4 * RC), BF),
        pltpu.VMEM((Y, X, 2, 2, RC, LANES), BF),
        dma((3,)),
        dma((2,)),
        dma,
        dma((Z,)),
        dma,
        dma((Y,)),
        dma,
        dma((2, Y // 2)),
        dma,
        dma((2,)),
        dma,
        dma((2,)),
        dma((2, 3)),
        dma((2, Y)),
        dma((2, Y // 2 + 1)),
        dma((2, Y // 2 + 1)),
    ]
    return pl.pallas_call(
        functools.partial(kernel, X, Y, Z, RC),
        out_shape=jax.ShapeDtypeStruct((rows, features), BF),
        in_specs=[hbm, hbm, hbm, smem, smem],
        out_specs=pl.BlockSpec(memory_space=pltpu.VMEM),
        scratch_shapes=scratch,
        compiler_params=pltpu.CompilerParams(
            collective_id=number, has_side_effects=True, vmem_limit_bytes=(18 + RC // 20) * 2**20
        ),
        name=f"step{RC}",
    )(hidden, weights, target, module, counts)


def choose(sizes, m_ref, n_ref, o_ref):
    paths = m_ref.shape[0]
    most = jnp.int32(0)
    for p in range(paths):
        total = jnp.int32(0)
        for q in range(paths):
            total = total + jnp.where(m_ref[q] == m_ref[p], (n_ref[q] + 3) // 4, 0)
        most = jnp.maximum(most, total)
    which = jnp.int32(0)
    for size in sizes[:-1]:
        which = which + jnp.where(most > size, 1, 0)
    o_ref[0] = which


def on_device(X, Y, Z, sizes, hidden, weights, target, module, counts):
    modules = module[:, 0]
    branches = [functools.partial(call, X, Y, Z, size, i) for i, size in enumerate(sizes)]
    operands = (hidden[0].T, weights[0], target[0].T, modules, counts)
    if len(sizes) == 1:
        return branches[0](*operands)[None]
    smem = pl.BlockSpec(memory_space=pltpu.SMEM)
    which = pl.pallas_call(
        functools.partial(choose, sizes),
        out_shape=jax.ShapeDtypeStruct((1,), jnp.int32),
        in_specs=[smem, smem],
        out_specs=smem,
        name="choose",
    )(modules, counts)
    return lax.switch(which[0], branches, *operands)[None]


def solution(mesh):
    in_specs = (
        P("group", None, "tensor"),
        P("group", "tensor", None),
        P("group", None, "tensor"),
        P(),
        P(),
    )
    return jax.shard_map(
        functools.partial(on_device, 4, 8, 12, SIZES),
        mesh=mesh, in_specs=in_specs, out_specs=P("group", "tensor", None), check_vma=False,
    )
```

```python
import functools
import math

import jax
import jax.numpy as jnp
from jax import lax
from jax.experimental import pallas as pl
from jax.experimental.pallas import tpu as pltpu
from jax.sharding import PartitionSpec as P

MESH = pl.DeviceIdType.MESH
BF = jnp.bfloat16
F32 = jnp.float32
LANES = 128
SIZES = (160, 192, 224, 448)


def kernel(X, Y, Z, RC, h_hbm, w_hbm, t_hbm, m_ref, n_ref, o_ref,
           h_ref, w_ref, t_ref, hp, tp, tr, hz, own, sibs, sibr, xs, xr, ys, yr, ez, pick, sel, hc, ea,
           load, t_sem, h_send, h_recv, sib_send, sib_recv, x_send, x_recv, y_send, y_recv, e_send, e_recv, a_send, a_recv, a_x, a_sib):
    z = lax.axis_index("group")
    t = lax.axis_index("tensor")
    x, y, c = t // (2 * Y), (t // 2) % Y, t % 2
    rows, tokens = h_ref.shape
    half = tokens // 2
    part = half // 2
    other = 1 - c

    def wrap(value, size):
        return lax.rem(value + 2 * size, size)

    def at(px, py, pz, pc):
        return (pz, (px * Y + py) * 2 + pc)

    def copy(src, dst, send, recv, device):
        return pltpu.make_async_remote_copy(
            src_ref=src, dst_ref=dst, send_sem=send, recv_sem=recv, device_id=device, device_id_type=MESH
        )

    sibling = at(x, y, z, other)
    loads = [
        pltpu.make_async_copy(source, target, load.at[i])
        for i, (source, target) in enumerate(((h_hbm, h_ref), (t_hbm, t_ref), (w_hbm, w_ref)))
    ]
    for item in loads:
        item.start()

    barrier = pltpu.get_barrier_semaphore()

    def greet(device):
        pl.semaphore_signal(barrier, inc=1, device_id=device, device_id_type=MESH)

    greet(sibling)
    for d in range(1, X):
        greet(at(wrap(x + d, X), y, z, c))
    for d in range(1, Y):
        greet(at(x, wrap(y + d, Y), z, c))
    for d in range(1, Z):
        greet(at(x, y, wrap(z + d, Z), c))

    slot = lax.broadcasted_iota(jnp.int32, (tokens, tokens), 0)
    token = lax.broadcasted_iota(jnp.int32, (tokens, tokens), 1)
    quarter = slot // part
    order = jnp.where(token == 4 * (slot % part) + 2 * (quarter % 2) + quarter // 2, 1.0, 0.0).astype(BF)
    loads[0].wait()
    loads[1].wait()
    by_last = (((1,), (1,)), ((), ()))
    hperm = lax.dot_general(order, h_ref[...], by_last, preferred_element_type=F32)
    hturn = lax.dot_general(h_ref[...], order, by_last, preferred_element_type=F32)
    tperm = lax.dot_general(order, t_ref[...], by_last, preferred_element_type=F32).astype(BF)
    twice = jnp.concatenate([tperm, tperm], axis=1)
    for k in range(2):
        hp[lax.rem(k + c, 2)] = hperm[k * half:(k + 1) * half].astype(BF)
        tp[k] = twice[k * half:(k + 1) * half]
        hz[z, k] = hturn[:, k * half:(k + 1) * half].astype(BF)

    pl.semaphore_wait(barrier, 1 + (X - 1) + (Y - 1) + (Z - 1))

    up, down = at(x, y, wrap(z + 1, Z), c), at(x, y, wrap(z - 1, Z), c)
    up_hops, down_hops = Z // 2, Z - 1 - Z // 2

    def hidden_copy(way, hop):
        source = wrap(z - (hop - 1), Z) if way == 0 else wrap(z + (hop - 1), Z)
        return copy(hz.at[source], hz.at[source], h_send, h_recv.at[source], up if way == 0 else down)

    def hidden_hop(hop):
        for way, hops in ((0, up_hops), (1, down_hops)):
            if 1 < hop <= hops + 1:
                source = wrap(z - (hop - 1), Z) if way == 0 else wrap(z + (hop - 1), Z)
                copy(hz.at[source], hz.at[source], h_send, h_recv.at[source], up).wait_recv()
            if hop <= hops:
                hidden_copy(way, hop).start()

    hidden_hop(1)
    target_copy = copy(tp.at[other], tr, t_sem.at[0], t_sem.at[1], sibling)
    target_copy.start()

    def sib_copy(k):
        return copy(sibs.at[k], sibr.at[k], sib_send, sib_recv.at[k], sibling)

    def partial_step(k, carry):
        to_y = wrap(y + 1 + k, Y)
        columns = jnp.concatenate(
            [w_ref[:, pl.ds(pl.multiple_of((i * Y + to_y) * LANES, LANES), LANES)] for i in range(X)], axis=1
        )
        both = jnp.dot(hp[...].reshape(tokens, rows), columns, preferred_element_type=F32)
        theirs = both[half:].astype(BF)
        for i in range(X):
            sibs[k, i] = theirs[:, i * LANES:(i + 1) * LANES]
        sib_copy(k).start()
        for i in range(X):
            own[k, i] = both[:half, i * LANES:(i + 1) * LANES]
        return carry

    loads[2].wait()
    lax.fori_loop(0, 2, partial_step, 0)

    def x_copy(p, m, d):
        pair = pl.ds(2 * m, 2)
        return copy(xs.at[p, pair, wrap(x + d, X)], xr.at[p, pair, d - 1], x_send, x_recv.at[p, m],
                    at(wrap(x + d, X), y, z, c))

    def x_step(m, carry):
        for n in range(2):
            k = 2 * m + n
            sib_copy(k).wait_recv()
            for i in range(X):
                value = own[k, i] + sibr[k, i].astype(F32)
                own[k, i] = value
                for p in range(2):
                    xs[p, k, i] = value[p * part:(p + 1) * part].astype(BF)
        for d in range(1, X):
            x_copy(0, m, d).start()
        return carry

    def pair_step(m, carry):
        for n in range(2):
            partial_step(2 * m + 2 + n, carry)
        return x_step(m, carry)

    lax.fori_loop(0, Y // 2 - 1, pair_step, 0)
    x_step(Y // 2 - 1, 0)

    def x_second(m, carry):
        for d in range(1, X):
            x_copy(1, m, d).start()
        return carry

    lax.fori_loop(0, Y // 2, x_second, 0)
    hidden_hop(2)

    my_module = m_ref[z]
    weight_sum = jnp.int32(0)
    live = []
    start = [jnp.int32(0)] * 4
    for q in range(Z):
        same = jnp.where(m_ref[q] == my_module, 1, 0)
        weight_sum = weight_sum + same * n_ref[q]
        entry = []
        for k in range(4):
            number = same * lax.div(n_ref[q] + 3 - k, 4)
            entry.append((start[k], number))
            start[k] = start[k] + number
        live.append(entry)
    share = jnp.full((1, LANES), n_ref[z], jnp.int32).astype(F32) / jnp.full((1, LANES), weight_sum, jnp.int32).astype(F32)


    row = lax.broadcasted_iota(jnp.int32, (RC, LANES), 0)
    lane = lax.broadcasted_iota(jnp.int32, (RC, LANES), 1)
    inner = lane % part
    gap = row - inner
    upper = lane >= part
    for k in range(2):
        for p in range(2):
            here = upper if p == 1 else jnp.logical_not(upper)
            for q in range(Z):
                first, number = live[q][2 * p + k]
                sel[k, p * RC:(p + 1) * RC, q * half:(q + 1) * half] = jnp.where(
                    (gap == first) & (inner < number) & here, 1.0, 0.0
                ).astype(BF)
    for p in range(2):
        for q in range(0, Z, 2):
            firsts, numbers = [], []
            for n in range(2):
                first, number = (jnp.where(c == 0, a, b) for a, b in zip(live[q + n][2 * p], live[q + n][2 * p + 1]))
                firsts.append(first)
                numbers.append(number)
            first = jnp.where(upper, firsts[1], firsts[0])
            number = jnp.where(upper, numbers[1], numbers[0])
            pick[p, :, q * part:(q + 2) * part] = jnp.where((gap == first) & (inner < number), 1.0, 0.0).astype(BF)

    def y_copy(p, k):
        return copy(ys.at[p, k], yr.at[p, k], y_send, y_recv.at[p], at(x, wrap(y + 1 + k, Y), z, c))

    def x_arrived(p, m):
        pair = xr.at[p, pl.ds(2 * m, 2)]
        copy(pair, pair, x_send, x_recv.at[p, m], sibling).wait_recv()

    def x_sum(p, k):
        value = own[k, x, p * part:(p + 1) * part]
        for d in range(1, X):
            value = value + xr[p, k, d - 1].astype(F32)
        return value

    def y_start(p, k):
        ys[p, k] = x_sum(p, k).astype(BF)
        y_copy(p, k).start()

    def y_step(p, m, carry):
        x_arrived(p, m)
        for n in range(2):
            y_start(p, 2 * m + n)
        return carry

    def y_last(p):
        x_arrived(p, Y // 2 - 1)
        y_start(p, Y - 2)

    def e_copy(p, d):
        return copy(ez.at[p, z], ez.at[p, z], e_send, e_recv.at[p], at(x, y, wrap(z + d, Z), c))

    def error_part(p):
        total = x_sum(p, Y - 1)
        copy(yr.at[p], yr.at[p], y_send, y_recv.at[p], sibling).wait_recv()
        for k in range(Y - 1):
            total = total + yr[p, k].astype(F32)
        mine, theirs = (ref[p * part:(p + 1) * part].astype(F32) for ref in (tp.at[c], tr))
        low = jnp.where(c == 0, mine, theirs)
        high = jnp.where(c == 0, theirs, mine)
        lane = lax.broadcasted_iota(jnp.int32, (part, LANES), 1)
        target = jnp.where(lane < LANES // 2, low, high)
        ez[p, z] = ((total - target) * (1.0 / math.sqrt(tokens)) * share).astype(BF)
        for d in [k // 2 + 1 if k % 2 == 0 else Z - 1 - k // 2 for k in range(Z - 1)]:
            e_copy(p, d).start()

    lax.fori_loop(0, Y // 2 - 1, functools.partial(y_step, 0), 0)
    hidden_hop(3)
    y_last(0)
    lax.fori_loop(0, Y // 2 - 2, functools.partial(y_step, 1), 0)
    target_copy.wait_recv()
    error_part(0)
    lax.fori_loop(Y // 2 - 2, Y // 2 - 1, functools.partial(y_step, 1), 0)
    y_last(1)
    error_part(1)

    rounds = Y // 2
    everyone = pl.ds(0, X)

    def place(hop, way):
        return min(2 * hop - 1 + way, Y - 1)

    def ring(hop):
        if hop == 0:
            return pl.ds(0, 1)
        return pl.ds(2 * hop - 1, 2) if hop < rounds else pl.ds(Y - 1, 1)

    def ways(p, core, hop):
        if hop > rounds:
            return ()
        return (0, 1) if hop < rounds else ((p + core) % 2,)

    def along_y(p, core, hop):
        columns = everyone if core == 0 else pl.ds(0, 1)
        for way in ways(p, core, hop):
            before = 0 if hop == 1 else place(hop - 1, way)
            after = place(hop, way)
            copy(ea.at[before, columns, core, p], ea.at[after, columns, core, p], a_send.at[p, 0], a_recv.at[p, after],
                 at(x, wrap(y + 1 - 2 * way, Y), z, c)).start()

    def y_arrived(p, core, hop):
        columns = everyone if core == 0 else pl.ds(0, 1)
        for way in ways(p, core, hop):
            block = ea.at[place(hop, way), columns, core, p]
            copy(block, block, a_send.at[p, 0], a_recv.at[p, place(hop, way)], sibling).wait_recv()

    def along_x(p, core, hop):
        for d in range(1, X):
            copy(ea.at[ring(hop), 0, core, p], ea.at[ring(hop), d, core, p], a_send.at[p, 2], a_x.at[p, hop],
                 at(wrap(x + d, X), y, z, c)).start()

    def x_blocks_arrived(p, core, hop):
        blocks = ea.at[ring(hop), pl.ds(1, X - 1), core, p]
        copy(blocks, blocks, a_send.at[p, 2], a_x.at[p, hop], sibling).wait_recv()

    def hand_over(p, core, hop):
        blocks = ea.at[ring(hop), everyone, core, p]
        copy(blocks, blocks, a_send.at[p, 1], a_sib.at[p, hop], sibling).start()

    def keep_hidden():
        kept = []
        for k in range(2):
            wide = jnp.concatenate([hz[q, k] for q in range(Z)], axis=1)
            kept.append(lax.dot_general(wide, sel[k], by_last, preferred_element_type=F32).astype(BF))
        hc[...] = jnp.concatenate(kept, axis=1)

    def keep_errors(p):
        others = ez.at[p, pl.ds(0, Z - 1)]
        copy(others, others, e_send, e_recv.at[p], sibling).wait_recv()
        errors = ez[p].reshape(Z * part, LANES)
        ea[0, 0, c, p] = jnp.dot(pick[p], errors, preferred_element_type=F32).astype(BF)

    def origin(p):
        keep_errors(p)

        @pl.when(c == 0)
        def _():
            along_x(p, 0, 0)

        @pl.when(c == 1)
        def _():
            along_y(p, 1, 1)
            along_x(p, 1, 0)

    def first(p):
        @pl.when(c == 0)
        def _():
            x_blocks_arrived(p, 0, 0)
            along_y(p, 0, 1)
            hand_over(p, 0, 0)

        @pl.when(c == 1)
        def _():
            y_arrived(p, 1, 1)
            along_y(p, 1, 2)
            along_x(p, 1, 1)

    def further(p, hop):
        @pl.when(c == 0)
        def _():
            y_arrived(p, 0, hop)
            along_y(p, 0, hop + 1)
            hand_over(p, 0, hop)

        @pl.when(c == 1)
        def _():
            if hop < rounds:
                y_arrived(p, 1, hop + 1)
                along_y(p, 1, hop + 2)
                along_x(p, 1, hop + 1)
            x_blocks_arrived(p, 1, hop - 1)
            hand_over(p, 1, hop - 1)
            if hop == rounds:
                x_blocks_arrived(p, 1, hop)
                hand_over(p, 1, hop)

    origin(0)
    first(0)
    origin(1)
    hidden_hop(4)
    first(1)
    def out_step(n, carry):
        i, d = n // (X // 2), n % (X // 2) * 2
        right = jnp.concatenate([ea[i, d + m].reshape(4 * RC, LANES) for m in range(2)], axis=1)
        value = jnp.dot(hc[...], right, preferred_element_type=F32).astype(BF)
        py = wrap(y + (i + 1) // 2 * (1 - 2 * (i % 2)), Y)
        for m in range(2):
            j = wrap(x - d - m, X) * Y + py
            o_ref[:, pl.ds(pl.multiple_of(j * LANES, LANES), LANES)] = value[:, m * LANES:(m + 1) * LANES]
        return carry

    def out(hop):
        for p in range(2):
            blocks = ea.at[ring(hop), everyone, other, p]
            copy(blocks, blocks, a_send.at[p, 1], a_sib.at[p, hop], sibling).wait_recv()
        low = max(2 * hop - 1, 0)
        lax.fori_loop(low * (X // 2), min(2 * hop + 1, Y) * (X // 2), out_step, 0)

    for hop in range(1, rounds + 1):
        for p in range(2):
            further(p, hop)
        if hop < rounds:
            hidden_hop(hop + 4)
        if hop == 3:
            keep_hidden()
        if hop == rounds - 1:
            for done in range(rounds - 1):
                out(done)
    for done in range(rounds - 1, rounds + 1):
        out(done)

    def sent(bytes_of, semaphore):
        copy(bytes_of, bytes_of, semaphore, t_sem.at[1], sibling).wait_send()

    sent(tr, t_sem.at[0])
    sent(hz.at[pl.ds(0, Z - 1)], h_send)
    sent(sibs, sib_send)
    sent(xr, x_send)
    sent(ys, y_send)
    sent(ez.at[:, pl.ds(0, Z - 1)], e_send)
    for p in range(2):
        sent(ea.at[:, :, c, p], a_send.at[p, 1])

        @pl.when(c == 0)
        def _(p=p):
            sent(ea.at[pl.ds(0, Y - 1), :, 0, p], a_send.at[p, 0])
            sent(ea.at[0, pl.ds(0, X - 1), 0, p], a_send.at[p, 2])

        @pl.when(c == 1)
        def _(p=p):
            sent(ea.at[pl.ds(0, Y - 1), 0, 1, p], a_send.at[p, 0])
            sent(ea.at[:, pl.ds(0, X - 1), 1, p], a_send.at[p, 2])


def call(X, Y, Z, RC, number, hidden, weights, target, module, counts):
    rows, tokens = hidden.shape
    features = weights.shape[1]
    half = tokens // 2
    part = half // 2
    hbm = pl.BlockSpec(memory_space=pl.ANY)
    smem = pl.BlockSpec(memory_space=pltpu.SMEM)
    dma = pltpu.SemaphoreType.DMA
    scratch = [
        pltpu.VMEM(hidden.shape, BF),
        pltpu.VMEM(weights.shape, BF),
        pltpu.VMEM(target.shape, BF),
        pltpu.VMEM((2, half, rows), BF),
        pltpu.VMEM((2, half, LANES), BF),
        pltpu.VMEM((half, LANES), BF),
        pltpu.VMEM((Z, 2, rows, half), BF),
        pltpu.VMEM((Y, X, half, LANES), F32),
        pltpu.VMEM((Y, X, half, LANES), BF),
        pltpu.VMEM((Y, X, half, LANES), BF),
        pltpu.VMEM((2, Y, X, part, LANES), BF),
        pltpu.VMEM((2, Y, X - 1, part, LANES), BF),
        pltpu.VMEM((2, Y - 1, part, LANES), BF),
        pltpu.VMEM((2, Y - 1, part, LANES), BF),
        pltpu.VMEM((2, Z, part, LANES), BF),
        pltpu.VMEM((2, RC, Z * part), BF),
        pltpu.VMEM((2, 2 * RC, Z * half), BF),
        pltpu.VMEM((rows, 4 * RC), BF),
        pltpu.VMEM((Y, X, 2, 2, RC, LANES), BF),
        dma((3,)),
        dma((2,)),
        dma,
        dma((Z,)),
        dma,
        dma((Y,)),
        dma,
        dma((2, Y // 2)),
        dma,
        dma((2,)),
        dma,
        dma((2,)),
        dma((2, 3)),
        dma((2, Y)),
        dma((2, Y // 2 + 1)),
        dma((2, Y // 2 + 1)),
    ]
    return pl.pallas_call(
        functools.partial(kernel, X, Y, Z, RC),
        out_shape=jax.ShapeDtypeStruct((rows, features), BF),
        in_specs=[hbm, hbm, hbm, smem, smem],
        out_specs=pl.BlockSpec(memory_space=pltpu.VMEM),
        scratch_shapes=scratch,
        compiler_params=pltpu.CompilerParams(
            collective_id=number, has_side_effects=True, vmem_limit_bytes=(18 + RC // 20) * 2**20
        ),
        name=f"step{RC}",
    )(hidden, weights, target, module, counts)


def choose(sizes, m_ref, n_ref, o_ref):
    paths = m_ref.shape[0]
    most = jnp.int32(0)
    for p in range(paths):
        total = jnp.int32(0)
        for q in range(paths):
            total = total + jnp.where(m_ref[q] == m_ref[p], (n_ref[q] + 3) // 4, 0)
        most = jnp.maximum(most, total)
    which = jnp.int32(0)
    for size in sizes[:-1]:
        which = which + jnp.where(most > size, 1, 0)
    o_ref[0] = which


def on_device(X, Y, Z, sizes, hidden, weights, target, module, counts):
    modules = module[:, 0]
    branches = [functools.partial(call, X, Y, Z, size, i) for i, size in enumerate(sizes)]
    operands = (hidden[0].T, weights[0], target[0].T, modules, counts)
    if len(sizes) == 1:
        return branches[0](*operands)[None]
    smem = pl.BlockSpec(memory_space=pltpu.SMEM)
    which = pl.pallas_call(
        functools.partial(choose, sizes),
        out_shape=jax.ShapeDtypeStruct((1,), jnp.int32),
        in_specs=[smem, smem],
        out_specs=smem,
        name="choose",
    )(modules, counts)
    return lax.switch(which[0], branches, *operands)[None]


def solution(mesh):
    in_specs = (
        P("group", None, "tensor"),
        P("group", "tensor", None),
        P("group", None, "tensor"),
        P(),
        P(),
    )
    return jax.shard_map(
        functools.partial(on_device, 4, 8, 12, SIZES),
        mesh=mesh, in_specs=in_specs, out_specs=P("group", "tensor", None), check_vma=False,
    )
```
